32 devices in a mesh: groups: 2 (over y), pb: 8 (over z, core), fc: 2 (over x), br: 1.
Axes of the slice: x: 2, y: 2, z: 4, core: 2. Of those that a mesh axis runs over, the one named last changes fastest.
Arguments:
- eigen_vectors: bfloat16 [64, 288, 288], P(('groups', 'pb'), 'br'), parts along dimension 0, may hold values from -0.375 to 0.375
- frequencies: bfloat16 [64, 288], P(('groups', 'pb'), 'br'), parts along dimension 0, may hold values from 0.35 to 0.49
- force_consts: bfloat16 [96, 3, 576], replicated, may hold values from -40 to 40
- neighbors: int32 [96, 8], replicated, may hold values from 0 to 95
- rotations: int32 [48, 3, 3], replicated, may hold values from -1 to 1, as said below
- atom_maps: int32 [48, 96], replicated, may hold values from 0 to 95, each once within a row
- grid_counts: int32 [16], P('groups'), parts along dimension 0, may hold values from 1 to 3, 12 in all
- trip_partners: int32 [24, 2], P('groups'), parts along dimension 0, may hold values from 1 to 31, as said below
- trip_turns: int32 [24, 2], P('groups'), parts along dimension 0, may hold values from 0 to 47
- trip_weights: int32 [24], P('groups'), parts along dimension 0, may hold values from 1 to 8
Outputs:
- linewidths: float32 [16, 288], P(('groups', 'pb')), parts along dimension 0
The draws below stay inside these ranges and needn't reach their ends.
There are 2 independent parts, one for each index of `groups`. The reference program is written for one: setup_inputs(seed, part) draws one part's arguments, and reference() takes and returns one part's arrays. A program takes and returns all parts, laid end to end along the dimension named above; an argument that names none is the same for every part. Nothing has to cross between parts.
Inputs may be any that keep to these rules, and one draw needn't show every extreme that they name: Each grid point has at least one triplet; the triplets of grid point g are rows start[g] to start[g] + grid_counts[g] - 1 of the triplet tables; the counts sum to 12. `trip_partners`: every table index that is not a multiple of 4 is named exactly once; multiples of 4 are grid points and are never partners. `rotations`: each matrix is a signed permutation of the three axes. `atom_maps`: each row is a permutation of the atoms.
All inputs are finite; a program needn't handle non-finite values.
Results may differ from the reference program's by a relative error of at most 0.0003.
Values may be sent and summed in bfloat16 or wider, within the bound.
A program may use at most 128 MiB of HBM per device.

```python
import math
import jax
import jax.numpy as jnp
import numpy as np
from jax import lax

ATOMS = 96
COMPS = 288
MODES = 288
NB = 8
NBC = 24
NROT = 48
QP_DEV = 4
CAP = 3
GRID = 8
NTRIP = 12
QPTS = 32


def draw_rotations(key, part):
    key = jax.random.fold_in(key, 7)
    order_key, sign_key = jax.random.split(key)
    subkeys = jax.random.split(order_key, NROT)
    orderings = jax.vmap(lambda subkey: jax.random.permutation(subkey, 3))(subkeys)
    sign_draw = jax.random.randint(sign_key, (NROT, 3), 0, 2) * 2 - 1
    places = jnp.arange(3)
    picked = (orderings[:, :, None] == places[None, None, :]).astype(jnp.int32)
    return (sign_draw[:, :, None] * picked).astype(jnp.int32)


def draw_trip_partners(key, part):
    key = jax.random.fold_in(key, 11)
    ordering = jax.random.permutation(key, 2 * NTRIP)
    per_owner = QP_DEV - 1
    mapped = ordering // per_owner * QP_DEV + 1 + ordering % per_owner
    return mapped.reshape(NTRIP, 2).astype(jnp.int32)


def draw_frequencies(key, part):
    key = jax.random.fold_in(key, 13)
    entry_key = jax.random.fold_in(key, 1)
    entries = jax.random.uniform(entry_key, (QPTS, MODES), jnp.float32)
    fraction = entries
    row_ids = jnp.arange(QPTS, dtype=jnp.int32)[:, None]
    is_grid = row_ids % QP_DEV == 0
    values = jnp.where(is_grid, 0.36 + 0.08 * fraction, 0.4 + 0.08 * fraction)
    return values.astype(jnp.bfloat16)


def draw_force_consts(key, part):
    key = jax.random.fold_in(key, 17)
    values = 8.0 * jax.random.truncated_normal(key, -5.0, 5.0, (ATOMS, 3, NBC * NBC), jnp.float32)
    return values.astype(jnp.bfloat16)


def plant(values, stream_key, smallest, high):
    longest = values.shape.index(max(values.shape))
    spots = []
    for shift in (0, 1):
        where = [jax.random.randint(jax.random.fold_in(stream_key, axis), (), 0, length) for axis, length in enumerate(values.shape)]
        where[longest] = (where[longest] + shift) % values.shape[longest]
        spots.append(tuple(where))
    return values.at[spots[0]].set(smallest).at[spots[1]].set(high)


def levels(own_key, dims, cuts, low, largest):
    loudness = 1.0
    for position, parts in cuts:
        draws = jax.random.uniform(jax.random.fold_in(jax.random.fold_in(own_key, 6), position), (parts,), jnp.float32, low / len(cuts), largest / len(cuts))
        loudness = loudness * jnp.repeat(jnp.exp(draws), dims[position] // parts).reshape((-1,) + (1,) * (len(dims) - 1 - position))
    return loudness


def split_up(count, total, limit, skew):
    weights = [(1 << 20) // math.isqrt(standing ** skew) + 1 for standing in range(2, count + 1)]
    rest, holding = total - limit - (count - 1), [1] * (count - 1)
    while rest > 0:
        candidates = [i for i in range(count - 1) if holding[i] < limit]
        pool, left = sum([weights[i] for i in candidates]), rest
        for i in candidates:
            addition = min(limit - holding[i], max(1, left * weights[i] // pool), rest)
            holding[i] = holding[i] + addition
            rest = rest - addition
    return np.array([limit] + holding)


def ragged_sizes(rng, number_of, total, most, lean):
    if number_of == 2:
        one = jax.random.randint(rng, (), max(1, total - most), min(most, total - 1) + 1)
        return jnp.stack([one, total - one])
    lengths = jnp.asarray(split_up(number_of, total, most, lean), jnp.int32)
    pairs = (number_of - 1) // 2
    source_of, receiver = lengths[1:1 + 2 * pairs:2], lengths[2:2 + 2 * pairs:2]
    slack = jnp.minimum(source_of - 1, most - receiver)
    shifted = jax.random.randint(jax.random.fold_in(rng, 1), (pairs,), 0, 1 << 20) % (slack + 1)
    lengths = lengths.at[1:1 + 2 * pairs:2].set(source_of - shifted).at[2:2 + 2 * pairs:2].set(receiver + shifted)
    return lengths[jax.random.permutation(jax.random.fold_in(rng, 2), number_of)]


def centred(stream_key, shape, deviation, limit, shards=(), held_as=jnp.bfloat16):
    gain = levels(stream_key, shape, shards, -0.22, 0.18) if shards else 1.0
    values = jax.random.normal(stream_key, shape, jnp.float32) * deviation * gain
    return jnp.minimum(jnp.maximum(values, -limit), limit).astype(held_as)


def setup_inputs(seed: int = 0, part: int = 0) -> dict:
    arg_keys = jax.random.split(jax.random.key(seed), 11)
    part_keys = jax.random.split(jax.random.fold_in(arg_keys[10], part), 11)
    eigen_vectors = centred(part_keys[0], (QPTS, MODES, COMPS), COMPS ** -0.5, 0.375, ((0, 8),))
    frequencies = draw_frequencies(jax.random.fold_in(jax.random.fold_in(arg_keys[10], part), 71), part)
    force_consts = draw_force_consts(jax.random.fold_in(arg_keys[10], 71), part)
    neighbors = plant(jax.random.randint(arg_keys[3], (ATOMS, NB), 0, ATOMS), jax.random.fold_in(arg_keys[3], 1), 0, ATOMS - 1).astype(jnp.int32)
    rotations = draw_rotations(jax.random.fold_in(arg_keys[10], 71), part)
    atom_maps = jax.vmap(lambda own: jax.random.permutation(own, ATOMS))(jax.random.split(arg_keys[5], NROT)).reshape((NROT, ATOMS)).astype(jnp.int32)
    grid_counts = ragged_sizes(part_keys[6], GRID, NTRIP, CAP, 2).astype(jnp.int32)
    trip_partners = draw_trip_partners(jax.random.fold_in(jax.random.fold_in(arg_keys[10], part), 71), part)
    trip_turns = plant(jax.random.randint(part_keys[8], (NTRIP, 2), 0, NROT), jax.random.fold_in(part_keys[8], 1), 0, NROT - 1).astype(jnp.int32)
    trip_weights = plant(jax.random.randint(part_keys[9], (NTRIP,), 1, 9), jax.random.fold_in(part_keys[9], 1), 1, 8).astype(jnp.int32)
    return dict(eigen_vectors=eigen_vectors, frequencies=frequencies, force_consts=force_consts, neighbors=neighbors, rotations=rotations, atom_maps=atom_maps, grid_counts=grid_counts, trip_partners=trip_partners, trip_turns=trip_turns, trip_weights=trip_weights)


SMEAR_WIDTH = 0.1

def smearing(offset):
    return jnp.exp(-0.5 * (offset / SMEAR_WIDTH) ** 2) / (SMEAR_WIDTH * math.sqrt(2.0 * math.pi))

def occupation(omega):
    return 1.0 / jnp.expm1(omega)

def kernel_terms(coupling, home_freq, left_freq, right_freq):
    left_occ = occupation(left_freq)[None, :, None]
    right_occ = occupation(right_freq)[None, None, :]
    home_omega = home_freq[:, None, None]
    left_omega = left_freq[None, :, None]
    right_omega = right_freq[None, None, :]
    weighting = (left_occ + right_occ + 1.0) * (smearing(home_omega - left_omega - right_omega) - smearing(home_omega + left_omega + right_omega))
    weighting = weighting + (left_occ - right_occ) * (smearing(home_omega + left_omega - right_omega) - smearing(home_omega - left_omega + right_omega))
    return lax.optimization_barrier(jnp.sum(coupling * coupling * weighting / (left_omega * right_omega), axis=(1, 2)))

def rotate(vectors, turned, mapping):
    atom_count = mapping.shape[0]
    matches = (jnp.arange(atom_count, dtype=jnp.int32)[:, None] == mapping[None, :]).astype(jnp.float32)
    axes_map = turned.astype(jnp.float32).T
    operator = (matches[:, None, :, None] * axes_map[None, :, None, :]).reshape(3 * atom_count, 3 * atom_count)
    return jnp.dot(vectors, operator.astype(jnp.bfloat16), preferred_element_type=jnp.float32).astype(jnp.bfloat16)

def neighbor_cols(vectors, neighbors):
    columns = (neighbors[:, :, None] * 3 + jnp.arange(3, dtype=jnp.int32)[None, None, :]).reshape(-1)
    return jnp.take(vectors, columns, axis=1).reshape(vectors.shape[0], neighbors.shape[0], -1)

def triplet_rate(home_vec, home_freq, left_vec, left_freq, right_vec, right_freq, force_consts, neighbors):
    atom_count = neighbors.shape[0]
    width = 3 * neighbors.shape[1]
    left_cols = neighbor_cols(left_vec, neighbors)
    right_cols = neighbor_cols(right_vec, neighbors)
    forces = force_consts.reshape(atom_count, 3, width, width)
    halfway = jnp.einsum('axnm,jam->axnj', forces.astype(jnp.float32), right_cols.astype(jnp.float32)).astype(jnp.bfloat16)
    block_rows = MODES // 4

    def one_block(block):
        left_block = lax.dynamic_slice_in_dim(left_cols, block * block_rows, block_rows, 0)
        freq_block = lax.dynamic_slice_in_dim(left_freq, block * block_rows, block_rows, 0)
        reduced = jnp.einsum('jan,axnk->axjk', left_block.astype(jnp.float32), halfway.astype(jnp.float32)).astype(jnp.bfloat16)
        coupling = jnp.dot(home_vec, reduced.reshape(3 * atom_count, -1), preferred_element_type=jnp.float32)
        coupling = coupling.reshape(home_vec.shape[0], block_rows, -1)
        return kernel_terms(coupling, home_freq, freq_block, right_freq)
    return lax.optimization_barrier(jnp.sum(lax.map(one_block, jnp.arange(4, dtype=jnp.int32)), axis=0))

def reference(eigen_vectors, frequencies, force_consts, neighbors, rotations, atom_maps, grid_counts, trip_partners, trip_turns, trip_weights):
    grid_count = grid_counts.shape[0]
    held_rows = eigen_vectors.shape[0] // grid_count
    starts = jnp.cumsum(grid_counts) - grid_counts
    prefactor = 16.0 / (MODES * MODES)

    def step(running, triple):
        owner = (jnp.sum((starts <= triple).astype(jnp.int32)) - 1).astype(jnp.int32)
        home_row = owner * held_rows
        home_vec = eigen_vectors[home_row]
        home_freq = frequencies[home_row].astype(jnp.float32)
        left_q = trip_partners[triple, 0]
        right_q = trip_partners[triple, 1]
        left_turn = trip_turns[triple, 0]
        right_turn = trip_turns[triple, 1]
        left_vec = rotate(eigen_vectors[left_q], rotations[left_turn], atom_maps[left_turn])
        right_vec = rotate(eigen_vectors[right_q], rotations[right_turn], atom_maps[right_turn])
        slot_rate = triplet_rate(home_vec, home_freq, left_vec, frequencies[left_q].astype(jnp.float32), right_vec, frequencies[right_q].astype(jnp.float32), force_consts, neighbors)
        slot_rate = slot_rate * (trip_weights[triple].astype(jnp.float32) * prefactor) / home_freq
        rows_hit = (jnp.arange(grid_count, dtype=jnp.int32) == owner).astype(jnp.float32)
        return (running + rows_hit[:, None] * slot_rate[None, :], None)
    running, _ = lax.scan(step, jnp.zeros((grid_count, MODES), jnp.float32), jnp.arange(trip_partners.shape[0], dtype=jnp.int32))
    return running
```

```python
import math

import jax
import jax.numpy as jnp
from jax import lax
from jax.experimental import pallas as pl
from jax.experimental.pallas import tpu as pltpu
from jax.sharding import PartitionSpec as P

SMEAR_WIDTH = 0.1
LEVELS = 128
GROUP = 8


def occupation(omega):
    return 1.0 / jnp.expm1(omega)


def columns_operator(turned, mapping, neighbors):
    atoms, slots = neighbors.shape
    target = mapping[neighbors]
    comp = jnp.arange(3 * atoms, dtype=jnp.int32)
    hit = target[:, :, None, None] == (comp // 3)[None, None, None, :]
    axes = jnp.tile(turned, (1, atoms))
    rows = jnp.where(hit, axes[None, None, :, :], 0)
    return rows.astype(jnp.bfloat16).reshape(3 * atoms * slots, 3 * atoms)


def unit_kernel(
    left_ref, right_ref, forces_ref, home_ref, at_ref, bt_ref, u1_ref, v1_ref, u2_ref, v2_ref,
    out_ref, half_main, half_tail, red_0, red_1, red_tail, squares, weights,
):
    atoms, rows, width = left_ref.shape[1:]
    comps = 3 * atoms
    modes = right_ref.shape[3]
    tail = modes - 256

    def halves(step, _):
        for inner in range(8):
            a = step * 8 + inner
            h = jnp.dot(forces_ref[a], right_ref[0, a], preferred_element_type=jnp.float32)
            parts = [h[x * width : (x + 1) * width] for x in range(3)]
            half_main[a] = jnp.concatenate([p[:, :256] for p in parts], axis=1).astype(jnp.bfloat16)
            ends = [p[:, 256:] for p in parts]
            ends.append(jnp.zeros((width, 128 - 3 * tail), jnp.float32))
            half_tail[a] = jnp.concatenate(ends, axis=1).astype(jnp.bfloat16)
        return 0

    lax.fori_loop(0, atoms // 8, halves, 0)

    def reduce_atoms(step, _):
        for inner in range(8):
            a = step * 8 + inner
            left = left_ref[0, a]
            main = jnp.dot(left, half_main[a], preferred_element_type=jnp.float32)
            ends = jnp.dot(left, half_tail[a], preferred_element_type=jnp.float32)
            for x in range(3):
                where = pl.ds(x * atoms + a, rows, stride=comps)
                red_0[where, :] = main[:, x * 256 : x * 256 + 128]
                red_1[where, :] = main[:, x * 256 + 128 : x * 256 + 256]
            red_tail[pl.ds(a, rows, stride=atoms), :] = ends
        return 0

    lax.fori_loop(0, atoms // 8, reduce_atoms, 0)

    def weigh(spot, a_col, b_col, u1, v1, u2, v2):
        q = u1 * (a_col * u2 - b_col * v2) + v1 * (b_col * u2 - a_col * v2)
        high = q.astype(jnp.bfloat16)
        low = (q - high.astype(jnp.float32)).astype(jnp.bfloat16)
        weights[spot, :LEVELS] = high
        weights[spot, LEVELS:] = low

    out_ref[0] = jnp.zeros(out_ref.shape[1:], jnp.float32)

    def group(g, _):
        home = home_ref[0]
        pieces = [[], [], []]
        for inner in range(GROUP):
            j = g * GROUP + inner
            a_col = at_ref[0, g][:, inner : inner + 1]
            b_col = bt_ref[0, g][:, inner : inner + 1]
            u1 = u1_ref[0, pl.ds(j, 1), :]
            v1 = v1_ref[0, pl.ds(j, 1), :]
            weigh(slice(inner * 256, inner * 256 + 256), a_col[:256], b_col[:256], u1, v1,
                  u2_ref[0, :256], v2_ref[0, :256])
            weigh(slice(GROUP * 256 + inner * tail, GROUP * 256 + (inner + 1) * tail),
                  a_col[256:], b_col[256:], u1, v1, u2_ref[0, 256:], v2_ref[0, 256:])
            base = pl.multiple_of(j * comps, comps)
            block = jnp.concatenate(
                [red_0[pl.ds(base, comps), :], red_1[pl.ds(base, comps), :]], axis=1
            ).astype(jnp.bfloat16)
            coupling = jnp.dot(home, block, preferred_element_type=jnp.float32)
            squares[:, inner * 256 : inner * 256 + 256] = (coupling * coupling).astype(jnp.bfloat16)
            ends = red_tail[pl.ds(pl.multiple_of(j * atoms, atoms), atoms), :]
            for x in range(3):
                pieces[x].append(ends[:, x * tail : (x + 1) * tail])
        block = jnp.concatenate(
            [jnp.concatenate(p, axis=1) for p in pieces], axis=0
        ).astype(jnp.bfloat16)
        coupling = jnp.dot(home, block, preferred_element_type=jnp.float32)
        squares[:, GROUP * 256 :] = (coupling * coupling).astype(jnp.bfloat16)
        out_ref[0] += jnp.dot(squares[...], weights[...], preferred_element_type=jnp.float32)
        return 0

    lax.fori_loop(0, rows // GROUP, group, 0)


def shards(
    eigen_vectors,
    frequencies,
    force_consts,
    neighbors,
    rotations,
    atom_maps,
    grid_counts,
    trip_partners,
    trip_turns,
    trip_weights,
):
    pb_count, fc_count, br_count = (lax.axis_size(n) for n in ("pb", "fc", "br"))
    devices = pb_count * fc_count * br_count
    me = (lax.axis_index("pb") * fc_count + lax.axis_index("fc")) * br_count + lax.axis_index("br")
    held = eigen_vectors.shape[0]
    modes = eigen_vectors.shape[1] * br_count
    comps = eigen_vectors.shape[2]
    atoms, slots = neighbors.shape
    width = 3 * slots
    trips = trip_weights.shape[0]
    common = math.gcd(trips, devices)
    cuts = devices // common
    units = trips // common
    block = modes // cuts
    rows = -(-block // GROUP) * GROUP
    groups = rows // GROUP
    f32 = jnp.float32

    table = lax.all_gather(eigen_vectors, "pb", axis=0, tiled=True)
    freq_table = lax.all_gather(frequencies, "pb", axis=0, tiled=True)
    if br_count > 1:
        table = lax.all_gather(table, "br", axis=1, tiled=True)
        freq_table = lax.all_gather(freq_table, "br", axis=1, tiled=True)

    starts = jnp.cumsum(grid_counts) - grid_counts
    ids = me * units + jnp.arange(units, dtype=jnp.int32)
    trip = ids // cuts
    first = ids % cuts * block
    owner = jnp.sum((starts[None, :] <= trip[:, None]).astype(jnp.int32), axis=1) - 1

    def rows_of(u):
        t = trip[u]
        left_q, right_q = trip_partners[t, 0], trip_partners[t, 1]
        left = lax.dynamic_slice(table, (left_q, first[u], 0), (1, block, comps))[0]
        left_f = lax.dynamic_slice(freq_table, (left_q, first[u]), (1, block))[0]
        home = lax.dynamic_index_in_dim(table, owner[u] * held, 0, False)
        home_f = lax.dynamic_index_in_dim(freq_table, owner[u] * held, 0, False)
        right = lax.dynamic_index_in_dim(table, right_q, 0, False)
        right_f = lax.dynamic_index_in_dim(freq_table, right_q, 0, False)
        return left, left_f, home, home_f, right, right_f

    picked = [jnp.stack(p) for p in zip(*[rows_of(u) for u in range(units)])]
    left, left_f, home, home_f, right, right_f = picked
    pad = rows - block
    if pad:
        left = jnp.pad(left, ((0, 0), (0, pad), (0, 0)))
        left_f = jnp.pad(left_f, ((0, 0), (0, pad)), mode="edge")

    turns = trip_turns[trip]
    operator = jax.vmap(columns_operator, (0, 0, None))
    left_op = operator(rotations[turns[:, 0]], atom_maps[turns[:, 0]], neighbors)
    right_op = operator(rotations[turns[:, 1]], atom_maps[turns[:, 1]], neighbors)
    left_cols = jnp.einsum("ujd,umd->ujm", left, left_op, preferred_element_type=f32)
    left_cols = left_cols.astype(jnp.bfloat16).reshape(units, rows, atoms, width).swapaxes(1, 2)
    right_cols = jnp.einsum("umd,ujd->umj", right_op, right, preferred_element_type=f32)
    right_cols = right_cols.astype(jnp.bfloat16).reshape(units, atoms, width, modes)

    sharp = 1.0 / (2.0 * SMEAR_WIDTH * SMEAR_WIDTH)
    level = (LEVELS + jnp.arange(LEVELS, dtype=f32)) / 512.0
    w1, w2, w0 = left_f.astype(f32), right_f.astype(f32), home_f.astype(f32)
    front = jnp.exp(-sharp * level * level) / (SMEAR_WIDTH * math.sqrt(2.0 * math.pi))
    u1 = front * jnp.exp(2.0 * sharp * w1[:, :, None] * level)
    v1 = front * jnp.exp(-2.0 * sharp * w1[:, :, None] * level)
    u2 = jnp.exp(2.0 * sharp * w2[:, :, None] * level)
    v2 = jnp.exp(-2.0 * sharp * w2[:, :, None] * level)
    w1g = w1.reshape(units, groups, 1, GROUP)
    w2g = w2[:, None, :, None]
    occ1, occ2 = occupation(w1g), occupation(w2g)
    at = (occ1 + occ2 + 1.0) * jnp.exp(-sharp * (w1g + w2g) ** 2) / (w1g * w2g)
    bt = (occ1 - occ2) * jnp.exp(-sharp * (w1g - w2g) ** 2) / (w1g * w2g)

    def spec(shape):
        return pl.BlockSpec((1,) + shape, lambda u: (u,) + (0,) * len(shape))

    n_cols = GROUP * modes
    sums = pl.pallas_call(
        unit_kernel,
        grid=(units,),
        in_specs=[
            spec((atoms, rows, width)),
            spec((atoms, width, modes)),
            pl.BlockSpec((atoms, 3 * width, width), lambda u: (0, 0, 0)),
            spec((modes, comps)),
            spec((groups, modes, GROUP)),
            spec((groups, modes, GROUP)),
            spec((rows, LEVELS)),
            spec((rows, LEVELS)),
            spec((modes, LEVELS)),
            spec((modes, LEVELS)),
        ],
        out_specs=spec((modes, 2 * LEVELS)),
        out_shape=jax.ShapeDtypeStruct((units, modes, 2 * LEVELS), f32),
        scratch_shapes=[
            pltpu.VMEM((atoms, width, 768), jnp.bfloat16),
            pltpu.VMEM((atoms, width, 128), jnp.bfloat16),
            pltpu.VMEM((rows * comps, 128), f32),
            pltpu.VMEM((rows * comps, 128), f32),
            pltpu.VMEM((rows * atoms, 128), f32),
            pltpu.VMEM((modes, n_cols), jnp.bfloat16),
            pltpu.VMEM((n_cols, 2 * LEVELS), jnp.bfloat16),
        ],
        compiler_params=pltpu.CompilerParams(vmem_limit_bytes=60 * 1024 * 1024),
    )(
        left_cols, right_cols, force_consts.reshape(atoms, 3 * width, width),
        jnp.concatenate([home[:, :, x::3] for x in range(3)], axis=2),
        at, bt, u1, v1, u2, v2,
    )
    folded = sums[:, :, :LEVELS] + sums[:, :, LEVELS:]
    mine = jnp.where(w0[:, :, None] == level, folded, 0.0)
    prefactor = 16.0 / (modes * modes)
    rates = jnp.sum(mine, axis=2) * (trip_weights[trip].astype(f32) * prefactor)[:, None] / w0
    hits = (jnp.arange(pb_count, dtype=jnp.int32)[:, None] == owner[None, :]).astype(f32)
    lines = jnp.sum(hits[:, :, None] * rates[None], axis=1)
    total = lax.psum(lines, ("pb", "fc", "br"))
    return lax.dynamic_slice_in_dim(total, lax.axis_index("pb"), 1, 0)


def solution(mesh):
    return jax.shard_map(
        shards,
        mesh=mesh,
        in_specs=(
            P(("groups", "pb"), "br", None),
            P(("groups", "pb"), "br"),
            P(),
            P(),
            P(),
            P(),
            P("groups"),
            P("groups", None),
            P("groups", None),
            P("groups"),
        ),
        out_specs=P(("groups", "pb"), None),
        check_vma=False,
    )
```

```python
import math

import jax
import jax.numpy as jnp
from jax import lax
from jax.experimental import pallas as pl
from jax.experimental.pallas import tpu as pltpu
from jax.sharding import PartitionSpec as P

SMEAR_WIDTH = 0.1
LEVELS = 128
GROUP = 8


def occupation(omega):
    return 1.0 / jnp.expm1(omega)


def columns_operator(turned, mapping, neighbors):
    atoms, slots = neighbors.shape
    axis = jnp.sum(jnp.abs(turned) * jnp.arange(3, dtype=jnp.int32), axis=1)
    sign = jnp.sum(turned, axis=1)
    target = mapping[neighbors.reshape(-1)]
    column = (target[:, None] * 3 + axis[None, :]).reshape(-1)
    signs = jnp.tile(sign, atoms * slots).astype(jnp.float32)
    comp = jnp.arange(3 * atoms, dtype=jnp.int32)
    return jnp.where(column[:, None] == comp[None, :], signs[:, None], 0.0).astype(jnp.bfloat16)


def exchange_sums(lines):
    for name in ("fc", "br"):
        hop = lax.axis_size(name) // 2
        while hop:
            pairs = [(i, i ^ hop) for i in range(lax.axis_size(name))]
            lines = lines + lax.ppermute(lines, name, pairs)
            hop //= 2
    place = lax.axis_index("pb")
    hop = lax.axis_size("pb") // 2
    while hop:
        pairs = [(i, i ^ hop) for i in range(lax.axis_size("pb"))]
        upper = (place & hop) != 0
        low, high = lines[:hop], lines[hop:]
        given = lax.ppermute(jnp.where(upper, low, high), "pb", pairs)
        lines = jnp.where(upper, high, low) + given
        hop //= 2
    return lines


def unit_kernel(
    left_ref, right_ref, forces_ref, home_ref, at_ref, bt_ref, u1_ref, v1_ref, u2_ref, v2_ref,
    out_ref, half_main, half_tail, red_0, red_1, red_tail, squares, weights,
):
    atoms, rows, width = left_ref.shape[1:]
    comps = 3 * atoms
    modes = right_ref.shape[3]
    tail = modes - 256

    def halves(step, _):
        for inner in range(8):
            a = step * 8 + inner
            h = jnp.dot(forces_ref[a], right_ref[0, a], preferred_element_type=jnp.float32)
            parts = [h[x * width : (x + 1) * width] for x in range(3)]
            half_main[a] = jnp.concatenate([p[:, :256] for p in parts], axis=1).astype(jnp.bfloat16)
            ends = [p[:, 256:] for p in parts]
            ends.append(jnp.zeros((width, 128 - 3 * tail), jnp.float32))
            half_tail[a] = jnp.concatenate(ends, axis=1).astype(jnp.bfloat16)
        return 0

    lax.fori_loop(0, atoms // 8, halves, 0)

    def reduce_atoms(step, _):
        for inner in range(8):
            a = step * 8 + inner
            left = left_ref[0, a]
            main = jnp.dot(left, half_main[a], preferred_element_type=jnp.float32)
            ends = jnp.dot(left, half_tail[a], preferred_element_type=jnp.float32)
            for x in range(3):
                where = pl.ds(x * atoms + a, rows, stride=comps)
                red_0[where, :] = main[:, x * 256 : x * 256 + 128]
                red_1[where, :] = main[:, x * 256 + 128 : x * 256 + 256]
            red_tail[pl.ds(a, rows, stride=atoms), :] = ends
        return 0

    lax.fori_loop(0, atoms // 8, reduce_atoms, 0)

    def weigh(spot, a_col, b_col, u1, v1, u2, v2):
        q = u1 * (a_col * u2 - b_col * v2) + v1 * (b_col * u2 - a_col * v2)
        high = q.astype(jnp.bfloat16)
        low = (q - high.astype(jnp.float32)).astype(jnp.bfloat16)
        weights[spot, :LEVELS] = high
        weights[spot, LEVELS:] = low

    out_ref[0] = jnp.zeros(out_ref.shape[1:], jnp.float32)

    def group(g, _):
        home = home_ref[0]
        pieces = [[], [], []]
        for inner in range(GROUP):
            j = g * GROUP + inner
            a_col = at_ref[0, g][:, inner : inner + 1]
            b_col = bt_ref[0, g][:, inner : inner + 1]
            u1 = u1_ref[0, pl.ds(j, 1), :]
            v1 = v1_ref[0, pl.ds(j, 1), :]
            weigh(slice(inner * 256, inner * 256 + 256), a_col[:256], b_col[:256], u1, v1,
                  u2_ref[0, :256], v2_ref[0, :256])
            weigh(slice(GROUP * 256 + inner * tail, GROUP * 256 + (inner + 1) * tail),
                  a_col[256:], b_col[256:], u1, v1, u2_ref[0, 256:], v2_ref[0, 256:])
            base = pl.multiple_of(j * comps, comps)
            block = jnp.concatenate(
                [red_0[pl.ds(base, comps), :], red_1[pl.ds(base, comps), :]], axis=1
            ).astype(jnp.bfloat16)
            coupling = jnp.dot(home, block, preferred_element_type=jnp.float32)
            squares[:, inner * 256 : inner * 256 + 256] = (coupling * coupling).astype(jnp.bfloat16)
            ends = red_tail[pl.ds(pl.multiple_of(j * atoms, atoms), atoms), :]
            for x in range(3):
                pieces[x].append(ends[:, x * tail : (x + 1) * tail])
        block = jnp.concatenate(
            [jnp.concatenate(p, axis=1) for p in pieces], axis=0
        ).astype(jnp.bfloat16)
        coupling = jnp.dot(home, block, preferred_element_type=jnp.float32)
        squares[:, GROUP * 256 :] = (coupling * coupling).astype(jnp.bfloat16)
        out_ref[0] += jnp.dot(squares[...], weights[...], preferred_element_type=jnp.float32)
        return 0

    lax.fori_loop(0, rows // GROUP, group, 0)


def shards(
    eigen_vectors,
    frequencies,
    force_consts,
    neighbors,
    rotations,
    atom_maps,
    grid_counts,
    trip_partners,
    trip_turns,
    trip_weights,
):
    pb_count, fc_count, br_count = (lax.axis_size(n) for n in ("pb", "fc", "br"))
    devices = pb_count * fc_count * br_count
    me = (lax.axis_index("pb") * fc_count + lax.axis_index("fc")) * br_count + lax.axis_index("br")
    held = eigen_vectors.shape[0]
    modes = eigen_vectors.shape[1] * br_count
    comps = eigen_vectors.shape[2]
    atoms, slots = neighbors.shape
    width = 3 * slots
    trips = trip_weights.shape[0]
    common = math.gcd(trips, devices)
    cuts = devices // common
    units = trips // common
    block = modes // cuts
    rows = -(-block // GROUP) * GROUP
    groups = rows // GROUP
    f32 = jnp.float32

    if br_count > 1:
        eigen_vectors = lax.all_gather(eigen_vectors, "br", axis=1, tiled=True)
        frequencies = lax.all_gather(frequencies, "br", axis=1, tiled=True)
    table = lax.all_gather(
        jnp.concatenate([eigen_vectors, frequencies[:, None, :]], axis=1), "pb", axis=0, tiled=True
    )

    starts = jnp.cumsum(grid_counts) - grid_counts
    ids = me * units + jnp.arange(units, dtype=jnp.int32)
    trip = ids // cuts
    first = ids % cuts * block
    owner = jnp.sum((starts[None, :] <= trip[:, None]).astype(jnp.int32), axis=1) - 1

    def rows_of(u):
        t = trip[u]
        left_q, right_q = trip_partners[t, 0], trip_partners[t, 1]
        left = lax.dynamic_slice(table, (left_q, first[u], 0), (1, block, comps))[0]
        left_f = lax.dynamic_slice(table, (left_q, modes, first[u]), (1, 1, block))[0, 0]
        home = lax.dynamic_slice(table, (owner[u] * held, 0, 0), (1, modes, comps))[0]
        home_f = lax.dynamic_slice(table, (owner[u] * held, modes, 0), (1, 1, modes))[0, 0]
        right = lax.dynamic_slice(table, (right_q, 0, 0), (1, modes, comps))[0]
        right_f = lax.dynamic_slice(table, (right_q, modes, 0), (1, 1, modes))[0, 0]
        return left, left_f, home, home_f, right, right_f

    picked = [jnp.stack(p) for p in zip(*[rows_of(u) for u in range(units)])]
    left, left_f, home, home_f, right, right_f = picked
    pad = rows - block
    if pad:
        left = jnp.pad(left, ((0, 0), (0, pad), (0, 0)))
        left_f = jnp.pad(left_f, ((0, 0), (0, pad)), mode="edge")

    comp = jnp.arange(comps, dtype=jnp.int32)
    order = comp[:, None] == (comp % atoms * 3 + comp // atoms)[None, :]
    home = jnp.einsum("ujc,cd->ujd", home, order.astype(jnp.bfloat16), preferred_element_type=f32)
    home = home.astype(jnp.bfloat16)

    turns = trip_turns[trip]
    operator = jax.vmap(columns_operator, (0, 0, None))
    left_op = operator(rotations[turns[:, 0]], atom_maps[turns[:, 0]], neighbors)
    right_op = operator(rotations[turns[:, 1]], atom_maps[turns[:, 1]], neighbors)
    left_cols = jnp.einsum("ujd,umd->ujm", left, left_op, preferred_element_type=f32)
    left_cols = left_cols.astype(jnp.bfloat16).reshape(units, rows, atoms, width).swapaxes(1, 2)
    right_cols = jnp.einsum("umd,ujd->umj", right_op, right, preferred_element_type=f32)
    right_cols = right_cols.astype(jnp.bfloat16).reshape(units, atoms, width, modes)

    sharp = 1.0 / (2.0 * SMEAR_WIDTH * SMEAR_WIDTH)
    level = (LEVELS + jnp.arange(LEVELS, dtype=f32)) / 512.0
    w1, w2, w0 = left_f.astype(f32), right_f.astype(f32), home_f.astype(f32)
    front = jnp.exp(-sharp * level * level) / (SMEAR_WIDTH * math.sqrt(2.0 * math.pi))
    u1 = front * jnp.exp(2.0 * sharp * w1[:, :, None] * level)
    v1 = front * jnp.exp(-2.0 * sharp * w1[:, :, None] * level)
    u2 = jnp.exp(2.0 * sharp * w2[:, :, None] * level)
    v2 = jnp.exp(-2.0 * sharp * w2[:, :, None] * level)
    w1g = w1.reshape(units, groups, 1, GROUP)
    w2g = w2[:, None, :, None]
    occ1, occ2 = occupation(w1g), occupation(w2g)
    at = (occ1 + occ2 + 1.0) * jnp.exp(-sharp * (w1g + w2g) ** 2) / (w1g * w2g)
    bt = (occ1 - occ2) * jnp.exp(-sharp * (w1g - w2g) ** 2) / (w1g * w2g)

    def spec(shape):
        return pl.BlockSpec((1,) + shape, lambda u: (u,) + (0,) * len(shape))

    n_cols = GROUP * modes
    sums = pl.pallas_call(
        unit_kernel,
        grid=(units,),
        in_specs=[
            spec((atoms, rows, width)),
            spec((atoms, width, modes)),
            pl.BlockSpec((atoms, 3 * width, width), lambda u: (0, 0, 0)),
            spec((modes, comps)),
            spec((groups, modes, GROUP)),
            spec((groups, modes, GROUP)),
            spec((rows, LEVELS)),
            spec((rows, LEVELS)),
            spec((modes, LEVELS)),
            spec((modes, LEVELS)),
        ],
        out_specs=spec((modes, 2 * LEVELS)),
        out_shape=jax.ShapeDtypeStruct((units, modes, 2 * LEVELS), f32),
        scratch_shapes=[
            pltpu.VMEM((atoms, width, 768), jnp.bfloat16),
            pltpu.VMEM((atoms, width, 128), jnp.bfloat16),
            pltpu.VMEM((rows * comps, 128), f32),
            pltpu.VMEM((rows * comps, 128), f32),
            pltpu.VMEM((rows * atoms, 128), f32),
            pltpu.VMEM((modes, n_cols), jnp.bfloat16),
            pltpu.VMEM((n_cols, 2 * LEVELS), jnp.bfloat16),
        ],
        compiler_params=pltpu.CompilerParams(vmem_limit_bytes=60 * 1024 * 1024),
    )(
        left_cols, right_cols, force_consts.reshape(atoms, 3 * width, width),
        home,
        at, bt, u1, v1, u2, v2,
    )
    folded = sums[:, :, :LEVELS] + sums[:, :, LEVELS:]
    mine = jnp.where(w0[:, :, None] == level, folded, 0.0)
    prefactor = 16.0 / (modes * modes)
    rates = jnp.sum(mine, axis=2) * (trip_weights[trip].astype(f32) * prefactor)[:, None] / w0
    hits = (jnp.arange(pb_count, dtype=jnp.int32)[:, None] == owner[None, :]).astype(f32)
    lines = jnp.sum(hits[:, :, None] * rates[None], axis=1)
    return exchange_sums(lines)


def solution(mesh):
    return jax.shard_map(
        shards,
        mesh=mesh,
        in_specs=(
            P(("groups", "pb"), "br", None),
            P(("groups", "pb"), "br"),
            P(),
            P(),
            P(),
            P(),
            P("groups"),
            P("groups", None),
            P("groups", None),
            P("groups"),
        ),
        out_specs=P(("groups", "pb"), None),
        check_vma=False,
    )
```

```python
import math

import jax
import jax.numpy as jnp
from jax import lax
from jax.experimental import pallas as pl
from jax.experimental.pallas import tpu as pltpu
from jax.sharding import PartitionSpec as P

SMEAR_WIDTH = 0.1
LEVELS = 128
GROUP = 8


def occupation(omega):
    return 1.0 / jnp.expm1(omega)


def columns_operator(turned, mapping, neighbors):
    atoms, slots = neighbors.shape
    axis = jnp.sum(jnp.abs(turned) * jnp.arange(3, dtype=jnp.int32), axis=1)
    sign = jnp.sum(turned, axis=1)
    target = mapping[neighbors.reshape(-1)]
    column = (target[:, None] * 3 + axis[None, :]).reshape(-1)
    signs = jnp.tile(sign, atoms * slots).astype(jnp.float32)
    comp = jnp.arange(3 * atoms, dtype=jnp.int32)
    return jnp.where(column[:, None] == comp[None, :], signs[:, None], 0.0).astype(jnp.bfloat16)


def exchange_sums(lines):
    for name in ("fc", "br"):
        hop = lax.axis_size(name) // 2
        while hop:
            pairs = [(i, i ^ hop) for i in range(lax.axis_size(name))]
            lines = lines + lax.ppermute(lines, name, pairs)
            hop //= 2
    place = lax.axis_index("pb")
    hop = lax.axis_size("pb") // 2
    while hop:
        pairs = [(i, i ^ hop) for i in range(lax.axis_size("pb"))]
        upper = (place & hop) != 0
        low, high = lines[:hop], lines[hop:]
        given = lax.ppermute(jnp.where(upper, low, high), "pb", pairs)
        lines = jnp.where(upper, high, low) + given
        hop //= 2
    return lines


def unit_kernel(
    left_ref, right_ref, forces_ref, home_ref, at_ref, bt_ref, u1_ref, v1_ref, u2_ref, v2_ref,
    out_ref, half_main, half_tail, red_0, red_1, red_tail, squares, weights,
):
    atoms, rows, width = left_ref.shape[1:]
    comps = 3 * atoms
    modes = right_ref.shape[3]
    tail = modes - 256

    def halves(step, _):
        for inner in range(16):
            a = step * 16 + inner
            right = right_ref[0, a].astype(jnp.bfloat16)
            h = jnp.dot(forces_ref[a], right, preferred_element_type=jnp.float32)
            parts = [h[x * width : (x + 1) * width] for x in range(3)]
            half_main[a] = jnp.concatenate([p[:, :256] for p in parts], axis=1).astype(jnp.bfloat16)
            ends = [p[:, 256:] for p in parts]
            ends.append(jnp.zeros((width, 128 - 3 * tail), jnp.float32))
            half_tail[a] = jnp.concatenate(ends, axis=1).astype(jnp.bfloat16)
        return 0

    lax.fori_loop(0, atoms // 16, halves, 0)

    def reduce_atoms(step, _):
        for inner in range(16):
            a = step * 16 + inner
            left = left_ref[0, a]
            main = jnp.dot(left, half_main[a], preferred_element_type=jnp.float32)
            ends = jnp.dot(left, half_tail[a], preferred_element_type=jnp.float32)
            for x in range(3):
                where = pl.ds(x * atoms + a, rows, stride=comps)
                red_0[where, :] = main[:, x * 256 : x * 256 + 128]
                red_1[where, :] = main[:, x * 256 + 128 : x * 256 + 256]
            red_tail[pl.ds(a, rows, stride=atoms), :] = ends
        return 0

    lax.fori_loop(0, atoms // 16, reduce_atoms, 0)

    def weigh(spot, a_col, b_col, u1, v1, u2, v2):
        q = u1 * (a_col * u2 - b_col * v2) + v1 * (b_col * u2 - a_col * v2)
        high = q.astype(jnp.bfloat16)
        low = (q - high.astype(jnp.float32)).astype(jnp.bfloat16)
        weights[spot, :LEVELS] = high
        weights[spot, LEVELS:] = low

    out_ref[0] = jnp.zeros(out_ref.shape[1:], jnp.float32)

    def group(g, _):
        home = home_ref[0]
        pieces = [[], [], []]
        for inner in range(GROUP):
            j = g * GROUP + inner
            a_col = at_ref[0, g][:, inner : inner + 1]
            b_col = bt_ref[0, g][:, inner : inner + 1]
            u1 = u1_ref[0, pl.ds(j, 1), :]
            v1 = v1_ref[0, pl.ds(j, 1), :]
            weigh(slice(inner * 256, inner * 256 + 256), a_col[:256], b_col[:256], u1, v1,
                  u2_ref[0, :256], v2_ref[0, :256])
            weigh(slice(GROUP * 256 + inner * tail, GROUP * 256 + (inner + 1) * tail),
                  a_col[256:], b_col[256:], u1, v1, u2_ref[0, 256:], v2_ref[0, 256:])
            base = pl.multiple_of(j * comps, comps)
            block = jnp.concatenate(
                [red_0[pl.ds(base, comps), :], red_1[pl.ds(base, comps), :]], axis=1
            ).astype(jnp.bfloat16)
            coupling = jnp.dot(home, block, preferred_element_type=jnp.float32)
            squares[:, inner * 256 : inner * 256 + 256] = (coupling * coupling).astype(jnp.bfloat16)
            ends = red_tail[pl.ds(pl.multiple_of(j * atoms, atoms), atoms), :]
            for x in range(3):
                pieces[x].append(ends[:, x * tail : (x + 1) * tail])
        block = jnp.concatenate(
            [jnp.concatenate(p, axis=1) for p in pieces], axis=0
        ).astype(jnp.bfloat16)
        coupling = jnp.dot(home, block, preferred_element_type=jnp.float32)
        squares[:, GROUP * 256 :] = (coupling * coupling).astype(jnp.bfloat16)
        out_ref[0] += jnp.dot(squares[...], weights[...], preferred_element_type=jnp.float32)
        return 0

    lax.fori_loop(0, rows // GROUP, group, 0)


def shards(
    eigen_vectors,
    frequencies,
    force_consts,
    neighbors,
    rotations,
    atom_maps,
    grid_counts,
    trip_partners,
    trip_turns,
    trip_weights,
):
    pb_count, fc_count, br_count = (lax.axis_size(n) for n in ("pb", "fc", "br"))
    devices = pb_count * fc_count * br_count
    me = (lax.axis_index("pb") * fc_count + lax.axis_index("fc")) * br_count + lax.axis_index("br")
    held = eigen_vectors.shape[0]
    modes = eigen_vectors.shape[1] * br_count
    comps = eigen_vectors.shape[2]
    atoms, slots = neighbors.shape
    width = 3 * slots
    trips = trip_weights.shape[0]
    common = math.gcd(trips, devices)
    cuts = devices // common
    units = trips // common
    block = modes // cuts
    rows = -(-block // GROUP) * GROUP
    groups = rows // GROUP
    f32 = jnp.float32

    if br_count > 1:
        eigen_vectors = lax.all_gather(eigen_vectors, "br", axis=1, tiled=True)
        frequencies = lax.all_gather(frequencies, "br", axis=1, tiled=True)
    table = lax.all_gather(
        jnp.concatenate([eigen_vectors, frequencies[:, None, :]], axis=1), "pb", axis=0, tiled=True
    )

    starts = jnp.cumsum(grid_counts) - grid_counts
    ids = me * units + jnp.arange(units, dtype=jnp.int32)
    trip = ids // cuts
    first = ids % cuts * block
    owner = jnp.sum((starts[None, :] <= trip[:, None]).astype(jnp.int32), axis=1) - 1

    def rows_of(u):
        t = trip[u]
        left_q, right_q = trip_partners[t, 0], trip_partners[t, 1]
        left = lax.dynamic_slice(table, (left_q, first[u], 0), (1, block, comps))[0]
        left_f = lax.dynamic_slice(table, (left_q, modes, first[u]), (1, 1, block))[0, 0]
        home = lax.dynamic_slice(table, (owner[u] * held, 0, 0), (1, modes, comps))[0]
        home_f = lax.dynamic_slice(table, (owner[u] * held, modes, 0), (1, 1, modes))[0, 0]
        right = lax.dynamic_slice(table, (right_q, 0, 0), (1, modes, comps))[0]
        right_f = lax.dynamic_slice(table, (right_q, modes, 0), (1, 1, modes))[0, 0]
        return left, left_f, home, home_f, right, right_f

    picked = [jnp.stack(p) for p in zip(*[rows_of(u) for u in range(units)])]
    left, left_f, home, home_f, right, right_f = picked
    pad = rows - block
    if pad:
        left = jnp.pad(left, ((0, 0), (0, pad), (0, 0)))
        left_f = jnp.pad(left_f, ((0, 0), (0, pad)), mode="edge")

    comp = jnp.arange(comps, dtype=jnp.int32)
    order = comp[:, None] == (comp % atoms * 3 + comp // atoms)[None, :]
    home = jnp.einsum("ujc,cd->ujd", home, order.astype(jnp.bfloat16), preferred_element_type=f32)
    home = home.astype(jnp.bfloat16)

    turns = trip_turns[trip]
    operator = jax.vmap(columns_operator, (0, 0, None))
    left_op = operator(rotations[turns[:, 0]], atom_maps[turns[:, 0]], neighbors)
    right_op = operator(rotations[turns[:, 1]], atom_maps[turns[:, 1]], neighbors)
    left_cols = jnp.einsum("ujd,umd->ujm", left, left_op, preferred_element_type=f32)
    left_cols = left_cols.astype(jnp.bfloat16).reshape(units, rows, atoms, width).swapaxes(1, 2)
    right_cols = jnp.einsum("umd,ujd->umj", right_op, right, preferred_element_type=f32)
    right_cols = right_cols.reshape(units, atoms, width, modes)

    sharp = 1.0 / (2.0 * SMEAR_WIDTH * SMEAR_WIDTH)
    level = (LEVELS + jnp.arange(LEVELS, dtype=f32)) / 512.0
    w1, w2, w0 = left_f.astype(f32), right_f.astype(f32), home_f.astype(f32)
    front = jnp.exp(-sharp * level * level) / (SMEAR_WIDTH * math.sqrt(2.0 * math.pi))
    u1 = front * jnp.exp(2.0 * sharp * w1[:, :, None] * level)
    v1 = front * jnp.exp(-2.0 * sharp * w1[:, :, None] * level)
    u2 = jnp.exp(2.0 * sharp * w2[:, :, None] * level)
    v2 = jnp.exp(-2.0 * sharp * w2[:, :, None] * level)
    w1g = w1.reshape(units, groups, 1, GROUP)
    w2g = w2[:, None, :, None]
    occ1, occ2 = occupation(w1g), occupation(w2g)
    at = (occ1 + occ2 + 1.0) * jnp.exp(-sharp * (w1g + w2g) ** 2) / (w1g * w2g)
    bt = (occ1 - occ2) * jnp.exp(-sharp * (w1g - w2g) ** 2) / (w1g * w2g)

    def spec(shape):
        return pl.BlockSpec((1,) + shape, lambda u: (u,) + (0,) * len(shape))

    n_cols = GROUP * modes
    sums = pl.pallas_call(
        unit_kernel,
        grid=(units,),
        in_specs=[
            spec((atoms, rows, width)),
            spec((atoms, width, modes)),
            pl.BlockSpec((atoms, 3 * width, width), lambda u: (0, 0, 0)),
            spec((modes, comps)),
            spec((groups, modes, GROUP)),
            spec((groups, modes, GROUP)),
            spec((rows, LEVELS)),
            spec((rows, LEVELS)),
            spec((modes, LEVELS)),
            spec((modes, LEVELS)),
        ],
        out_specs=spec((modes, 2 * LEVELS)),
        out_shape=jax.ShapeDtypeStruct((units, modes, 2 * LEVELS), f32),
        scratch_shapes=[
            pltpu.VMEM((atoms, width, 768), jnp.bfloat16),
            pltpu.VMEM((atoms, width, 128), jnp.bfloat16),
            pltpu.VMEM((rows * comps, 128), f32),
            pltpu.VMEM((rows * comps, 128), f32),
            pltpu.VMEM((rows * atoms, 128), f32),
            pltpu.VMEM((modes, n_cols), jnp.bfloat16),
            pltpu.VMEM((n_cols, 2 * LEVELS), jnp.bfloat16),
        ],
        compiler_params=pltpu.CompilerParams(vmem_limit_bytes=60 * 1024 * 1024),
    )(
        left_cols, right_cols, force_consts.reshape(atoms, 3 * width, width),
        home,
        at, bt, u1, v1, u2, v2,
    )
    folded = sums[:, :, :LEVELS] + sums[:, :, LEVELS:]
    mine = jnp.where(w0[:, :, None] == level, folded, 0.0)
    prefactor = 16.0 / (modes * modes)
    rates = jnp.sum(mine, axis=2) * (trip_weights[trip].astype(f32) * prefactor)[:, None] / w0
    hits = (jnp.arange(pb_count, dtype=jnp.int32)[:, None] == owner[None, :]).astype(f32)
    lines = jnp.sum(hits[:, :, None] * rates[None], axis=1)
    return exchange_sums(lines)


def solution(mesh):
    return jax.shard_map(
        shards,
        mesh=mesh,
        in_specs=(
            P(("groups", "pb"), "br", None),
            P(("groups", "pb"), "br"),
            P(),
            P(),
            P(),
            P(),
            P("groups"),
            P("groups", None),
            P("groups", None),
            P("groups"),
        ),
        out_specs=P(("groups", "pb"), None),
        check_vma=False,
    )
```
